256 devices in a mesh: row: 16 (over z, core), col: 16 (over y, x).
Axes of the slice: x: 4, y: 4, z: 8, core: 2. Of those that a mesh axis runs over, the one named last changes fastest.
Arguments:
- object_slices: float32 [2, 2, 4096, 4096], P(None, None, 'row', 'col'), may hold values from -5 to 5
- probe_wave: float32 [2, 256, 256], replicated, may hold values from -6 to 6
- propagator: float32 [2, 256, 256], replicated, may hold values from -5 to 5
- measured: float32 [16, 16, 4, 256, 256], P('row', 'col'), as said below
- positions: int32 [16, 16, 4, 2], P('row', 'col'), may hold values from -128 to 128, as said below
- scan_counts: int32 [16, 16], P('row', 'col'), may hold values from 1 to 4, as said below
Outputs:
- object_grad: float32 [2, 2, 4096, 4096], P(None, None, 'row', 'col')
- probe_grad: float32 [2, 256, 256], replicated
The draws below stay inside these ranges and needn't reach their ends.
Inputs may be any that keep to these rules, and one draw needn't show every extreme that they name: `positions`: every patch of 256 x 256 cells lies inside the object window. Slots k < scan_counts[r, c] of tile (r, c) are used, the others are ignored. `measured`: positive intensities.
All inputs are finite; a program needn't handle non-finite values.
Results may differ from the reference program's by a relative error of at most 0.0003.
Values sent between devices are 32-bit elements; how exact they have to be, the bound alone decides.
A program may use at most 128 MiB of HBM per device.

```python
import math
import jax
import jax.numpy as jnp
from jax import lax

W = 256
HALF = 128
SLICES = 2
TILE = 256
CAP = 4
NTR = 16
NTC = 16
OY = 4096
OX = 4096


def draw_scan_counts(key, part):
    key = jax.random.fold_in(key, 12)
    first_key, second_key, third_key = jax.random.split(key, 3)
    first = jax.random.randint(first_key, (NTR, NTC), 1, CAP + 1)
    second = jax.random.randint(second_key, (NTR, NTC), 1, CAP + 1)
    counted = jnp.minimum(first, second).reshape(-1)
    chosen = jax.random.randint(third_key, (), 0, NTR * NTC)
    counted = jnp.where(jnp.arange(NTR * NTC) == chosen, CAP, counted)
    return counted.reshape(NTR, NTC).astype(jnp.int32)


def draw_positions(key, part):
    key = jax.random.fold_in(key, 13)
    row_key, col_key = jax.random.split(key, 2)
    tile_row = jnp.arange(NTR, dtype=jnp.int32)[:, None, None]
    tile_col = jnp.arange(NTC, dtype=jnp.int32)[None, :, None]
    slot_at = jnp.arange(CAP, dtype=jnp.int32)[None, None, :]
    row_low = jnp.where(tile_row > 0, 0 - HALF, 0)
    row_high = jnp.where(tile_row < NTR - 1, TILE - HALF, TILE - W)
    col_low = jnp.where(tile_col > 0, 0 - HALF, 0)
    col_high = jnp.where(tile_col < NTC - 1, TILE - HALF, TILE - W)
    row_draw = jax.random.randint(row_key, (NTR, NTC, CAP), 0, 1 << 20)
    col_draw = jax.random.randint(col_key, (NTR, NTC, CAP), 0, 1 << 20)
    rows = row_low + row_draw % (row_high - row_low + 1)
    cols = col_low + col_draw % (col_high - col_low + 1)
    even = (tile_row + tile_col) % 2 == 0
    rows = jnp.where(slot_at == 0, jnp.where(even, row_low, row_high), rows)
    cols = jnp.where(slot_at == 0, jnp.where(even, col_high, col_low), cols)
    return jnp.stack((rows, cols), axis=-1).astype(jnp.int32)


def draw_measured(key, part):
    key = jax.random.fold_in(key, 14)
    pixel_key, pattern_key = jax.random.split(key, 2)
    tile_rows = jnp.arange(NTR, dtype=jnp.float32)[:, None, None, None, None]
    tile_scale = 1.0 + 2.0 * tile_rows / max(NTR - 1, 1)
    pattern = jnp.exp(jax.random.uniform(pattern_key, (NTR, NTC, CAP, 1, 1), dtype=jnp.float32) * math.log(10.0))
    pixels = jax.random.uniform(pixel_key, (NTR, NTC, CAP, W, W), dtype=jnp.float32, minval=0.2, maxval=2.0)
    return (tile_scale * pattern * pixels).astype(jnp.float32)


def steps_of(own_key, shape, cuts, low, top_value):
    def one(axis_at, parts):
        steps = jax.random.uniform(jax.random.fold_in(jax.random.fold_in(own_key, 6), axis_at), (parts,), jnp.float32, low / len(cuts), top_value / len(cuts))
        return jnp.repeat(jnp.exp(steps), shape[axis_at] // parts).reshape((-1,) + (1,) * (len(shape) - axis_at - 1))

    factor_of = one(*cuts[0])
    for cut in cuts[1:]:
        factor_of = factor_of * one(*cut)
    return factor_of


def normal_values(own_key, extent, scale, limit, cuts=(), kind=jnp.bfloat16):
    drawn = scale * jax.random.normal(own_key, extent, jnp.float32)
    if cuts:
        drawn = drawn * steps_of(own_key, extent, cuts, -0.22, 0.18)
    return jnp.clip(drawn, -limit, limit).astype(kind)


def setup_inputs(seed: int = 0) -> dict:
    splits = jax.random.split(jax.random.key(seed), 7)
    object_slices = normal_values(splits[0], (SLICES, 2, OY, OX), 0.7, 5.0, ((2, 16), (3, 16)), jnp.float32)
    probe_wave = normal_values(splits[1], (2, W, W), 1.0, 6.0, (), jnp.float32)
    propagator = normal_values(splits[2], (2, W, W), 0.7, 5.0, (), jnp.float32)
    measured = draw_measured(jax.random.fold_in(splits[6], 71), 0)
    positions = draw_positions(jax.random.fold_in(splits[6], 71), 0)
    scan_counts = draw_scan_counts(jax.random.fold_in(splits[6], 71), 0)
    return {"object_slices": object_slices, "probe_wave": probe_wave, "propagator": propagator, "measured": measured, "positions": positions, "scan_counts": scan_counts}


def forward_fft(field):
    return jnp.fft.fft2(field, norm="ortho")


def inverse_fft(field):
    return jnp.fft.ifft2(field, norm="ortho")


def slot_gradient(patch, probe_wave, propagator, target):
    kernel = lax.complex(propagator[0], propagator[1])
    wave = lax.complex(probe_wave[0], probe_wave[1])
    layers = patch.shape[0]
    incoming = []
    transmits = []
    for layer_at in range(layers):
        transmit = lax.complex(patch[layer_at, 0], patch[layer_at, 1])
        transmits.append(transmit)
        incoming.append(wave)
        exited = wave * transmit
        if layer_at + 1 < layers:
            wave = inverse_fft(kernel * forward_fft(exited))
    far_field = forward_fft(exited)
    misfit = jnp.real(far_field) * jnp.real(far_field) + jnp.imag(far_field) * jnp.imag(far_field) - target
    adjoint = inverse_fft(misfit * far_field)
    gradients = [None] * layers
    for layer_at in range(layers - 1, -1, -1):
        term = jnp.conj(incoming[layer_at]) * adjoint
        gradients[layer_at] = jnp.stack((jnp.real(term), jnp.imag(term)))
        adjoint = jnp.conj(transmits[layer_at]) * adjoint
        if layer_at > 0:
            adjoint = inverse_fft(jnp.conj(kernel) * forward_fft(adjoint))
    return jnp.stack(gradients), jnp.stack((jnp.real(adjoint), jnp.imag(adjoint)))


def reference(object_slices, probe_wave, propagator, measured, positions, scan_counts):
    float_type = object_slices.dtype
    padded = jnp.pad(object_slices, ((0, 0), (0, 0), (HALF, HALF), (HALF, HALF)))
    per_tile = NTC * CAP

    def visit(state_pair, flat_index):
        accum, probe_sum = state_pair
        tile_row = flat_index // per_tile
        tile_col = (flat_index // CAP) % NTC
        slot_at = flat_index % CAP
        offset = positions[tile_row, tile_col, slot_at]
        row_start = (tile_row * TILE + offset[0] + HALF).astype(jnp.int32)
        col_start = (tile_col * TILE + offset[1] + HALF).astype(jnp.int32)
        starts = (jnp.int32(0), jnp.int32(0), row_start, col_start)
        patch = lax.dynamic_slice(padded, starts, (SLICES, 2, W, W))
        gradients, adjoint = slot_gradient(patch, probe_wave, propagator, measured[tile_row, tile_col, slot_at])
        weight = (slot_at < scan_counts[tile_row, tile_col]).astype(float_type)
        region = lax.dynamic_slice(accum, starts, (SLICES, 2, W, W)) + weight * gradients
        accum = lax.dynamic_update_slice(accum, region, starts)
        return (accum, probe_sum + weight * adjoint), None

    initial = (jnp.zeros_like(padded), jnp.zeros((2, W, W), float_type))
    (accum, probe_sum), trailing = lax.scan(visit, initial, jnp.arange(NTR * NTC * CAP, dtype=jnp.int32))
    live = (jnp.arange(CAP, dtype=jnp.int32)[None, None, :] < scan_counts[:, :, None]).astype(float_type)
    total = jnp.sum(live * jnp.sum(measured, axis=(3, 4)))
    scans = jnp.sum(scan_counts).astype(float_type)
    mean_level = total / (scans * (W * W))
    object_grad = accum[:, :, HALF:HALF + OY, HALF:HALF + OX] / mean_level
    return object_grad, probe_sum / (mean_level * scans)
```

```python
import functools
import math

import jax
import jax.numpy as jnp
import ml_dtypes
import numpy as np
from jax import lax
from jax.experimental import pallas as pl
from jax.experimental.pallas import tpu as pltpu
from jax.sharding import PartitionSpec as P

F32, BF16 = jnp.float32, jnp.bfloat16
MESH = pl.DeviceIdType.MESH
EVEN, EVEN_T, ODD, ODD_T = 0, 2, 4, 6
CHUNK = 32


def split_table(table):
    high = table.astype(ml_dtypes.bfloat16)
    return [high, (table - high.astype(np.float64)).astype(ml_dtypes.bfloat16)]


def dft_tables(width):
    half = width // 2
    out = []
    for parity in range(2):
        k = np.arange(half)[:, None] * 2 + parity
        n = np.arange(half)[None, :]
        angle = 2.0 * math.pi * ((k * n) % width) / width
        c, s = np.cos(angle) / math.sqrt(width), np.sin(angle) / math.sqrt(width)
        block = np.block([[c, s], [-s, c]])
        out += split_table(block) + split_table(block.T)
    return np.stack(out)


def order_tables(width):
    half = width // 2
    order = np.concatenate([np.arange(half) * 2, np.arange(half) * 2 + 1])
    perm = np.zeros((width, width))
    perm[order, np.arange(width)] = 1.0
    return np.stack([perm, perm.T]).astype(ml_dtypes.bfloat16)


def cat(parts, axis):
    return jnp.concatenate(parts, axis=axis)


def split(x):
    high = x.astype(BF16)
    return high, (x - high.astype(F32)).astype(BF16)


def mm(a, b):
    return jnp.dot(a, b, preferred_element_type=F32)


def right(x, tables, at):
    high, low = split(x)
    th, tl = tables[at], tables[at + 1]
    return mm(high, th) + mm(low, th) + mm(high, tl)


def left(tables, at, x):
    high, low = split(x)
    th, tl = tables[at], tables[at + 1]
    return mm(th, high) + mm(th, low) + mm(tl, high)


def forward(re, im, tables):
    h = re.shape[1] // 2
    u = cat([re[:, :h] + re[:, h:], im[:, :h] + im[:, h:]], 1)
    v = cat([re[:, :h] - re[:, h:], im[:, :h] - im[:, h:]], 1)
    e, o = right(u, tables, EVEN_T), right(v, tables, ODD_T)
    es, os = e[:h] + e[h:], o[:h] + o[h:]
    ed, od = e[:h] - e[h:], o[:h] - o[h:]
    a = cat([cat([es[:, :h], os[:, :h]], 1), cat([es[:, h:], os[:, h:]], 1)], 0)
    b = cat([cat([ed[:, :h], od[:, :h]], 1), cat([ed[:, h:], od[:, h:]], 1)], 0)
    return left(tables, EVEN, a), left(tables, ODD, b)


def inverse(a, b, tables):
    h = a.shape[0] // 2
    e, o = left(tables, EVEN_T, a), left(tables, ODD_T, b)
    t, w = e + o, e - o
    qe = cat([cat([t[:h, :h], t[h:, :h]], 1), cat([w[:h, :h], w[h:, :h]], 1)], 0)
    qo = cat([cat([t[:h, h:], t[h:, h:]], 1), cat([w[:h, h:], w[h:, h:]], 1)], 0)
    e, o = right(qe, tables, EVEN), right(qo, tables, ODD)
    s, d = e + o, e - o
    return cat([s[:, :h], d[:, :h]], 1), cat([s[:, h:], d[:, h:]], 1)


def freq_mul(a, k, conj):
    h = a.shape[0] // 2
    kr, ki, ar, ai = k[:h], k[h:], a[:h], a[h:]
    if conj:
        return cat([kr * ar + ki * ai, kr * ai - ki * ar], 0)
    return cat([kr * ar - ki * ai, kr * ai + ki * ar], 0)


def reorder(x, order):
    high, low = split(x)
    high, low = split(mm(high, order[0]) + mm(low, order[0]))
    return mm(order[1], high) + mm(order[1], low)


def turn(x, down, along):
    return pltpu.roll(pltpu.roll(x, along, 1), down, 0)


def kernel(
    W, NR, NC,
    obj, probe, prop, meas, pos, cnt, tables, order,
    grad_out, probe_out,
    ext, gext, kperm, mperm, probes, waves, grads, psum,
    rbuf, cbuf, pieces, landed, tiles, tile_landed, tile_all, piece_all,
    own_sem, halo_send, halo_recv, grow_send, grow_recv, gcol_send, gcol_recv,
    rs_send, rs_recv, rt_send, rt_recv, ag_send, ag_recv, ac_send, ac_recv,
):
    h = W // 2
    cap = meas.shape[0]
    row, col = lax.axis_index("row"), lax.axis_index("col")
    up, down = lax.rem(row + NR - 1, NR), lax.rem(row + 1, NR)
    lft, rgt = lax.rem(col + NC - 1, NC), lax.rem(col + 1, NC)
    to_up, to_down, to_left, to_right = (up, col), (down, col), (row, lft), (row, rgt)
    piece_rows = 4 * W // NC
    zs = NR // 2
    tile_rows = piece_rows // zs

    def remote(src, dst, send, recv, device):
        return pltpu.make_async_remote_copy(
            src_ref=src, dst_ref=dst, send_sem=send, recv_sem=recv,
            device_id=device, device_id_type=MESH,
        )

    barrier = pltpu.get_barrier_semaphore()

    def greet_col(d, carry):
        pl.semaphore_signal(barrier, inc=1, device_id=(row, lax.rem(col + d, NC)), device_id_type=MESH)
        return carry

    def greet_row(d, carry):
        pl.semaphore_signal(barrier, inc=1, device_id=(lax.rem(row + d, NR), col), device_id_type=MESH)
        return carry

    lax.fori_loop(1, NC, greet_col, 0)
    lax.fori_loop(1, NR, greet_row, 0)
    own = pltpu.make_async_copy(obj, ext.at[:, :, h:h + W, h:h + W], own_sem)
    own.start()
    pl.semaphore_wait(barrier, NC + NR - 2)

    far = h + W
    halos = []
    for s in range(2):
        sides = []
        for q in range(2):
            here = pl.ds(q * h, h)
            there = pl.ds(h + q * h, h)
            for side in range(2):
                n = s * 10 + q * 2 + side
                src = obj.at[s, :, here, pl.ds(h, h)] if side == 0 else obj.at[s, :, here, pl.ds(0, h)]
                dst = ext.at[s, :, there, pl.ds(0, h)] if side == 0 else ext.at[s, :, there, pl.ds(far, h)]
                sides.append(remote(src, dst, halo_send.at[n], halo_recv.at[n], to_right if side == 0 else to_left))
        middles = [
            remote(obj.at[s, :, pl.ds(0, h), :], ext.at[s, :, pl.ds(far, h), pl.ds(h, W)],
                   halo_send.at[s * 10 + 4], halo_recv.at[s * 10 + 4], to_up),
            remote(obj.at[s, :, pl.ds(h, h), :], ext.at[s, :, pl.ds(0, h), pl.ds(h, W)],
                   halo_send.at[s * 10 + 5], halo_recv.at[s * 10 + 5], to_down),
        ]
        corners = []
        for q in range(2):
            for side in range(2):
                n = s * 10 + 6 + q * 2 + side
                lanes = pl.ds(0, h) if side == 0 else pl.ds(far, h)
                corners.append(remote(
                    ext.at[s, :, pl.ds(h + q * h, h), lanes],
                    ext.at[s, :, pl.ds(far, h) if q == 0 else pl.ds(0, h), lanes],
                    halo_send.at[n], halo_recv.at[n], to_up if q == 0 else to_down,
                ))
        halos.append((sides, middles, corners))
    for sides, middles, corners in halos:
        for c in sides + middles:
            c.start()

    def forward_corners(s):
        sides, middles, corners = halos[s]
        for side, corner in zip(sides, corners):
            side.wait_recv()
            corner.start()

    def finish_halo(s):
        sides, middles, corners = halos[s]
        for c in middles + corners:
            c.wait_recv()

    rows = lax.broadcasted_iota(jnp.int32, (W, W), 0)
    cols = lax.broadcasted_iota(jnp.int32, (W, W), 1)
    count = cnt[0]
    starts = [
        (jnp.clip(pos[2 * k] + h, 0, W), jnp.clip(pos[2 * k + 1] + h, 0, W)) for k in range(cap)
    ]
    kr, ki = reorder(prop[0], order), reorder(prop[1], order)
    kperm[0] = cat([kr[:h], ki[:h]], 0)
    kperm[1] = cat([kr[h:], ki[h:]], 0)

    def start_of(k):
        return jnp.clip(pos[2 * k] + h, 0, W), jnp.clip(pos[2 * k + 1] + h, 0, W)

    def prepare(k, total):
        r0, c0 = start_of(k)
        m = meas[k]
        mperm[k] = reorder(m, order)
        probes[k, 0] = turn(probe[0], lax.rem(r0, W), lax.rem(c0, W))
        probes[k, 1] = turn(probe[1], lax.rem(r0, W), lax.rem(c0, W))
        return total + jnp.where(k < count, jnp.sum(m.reshape(W // 8, 8, W), axis=0), 0.0)

    total = jnp.sum(lax.fori_loop(0, cap, prepare, jnp.zeros((8, W), F32)))
    first_rows = lax.broadcasted_iota(jnp.int32, (8, h), 0) < 4
    level = jnp.where(first_rows, total, count.astype(F32))

    def pick(k, s, ri):
        r0, c0 = start_of(k)
        inr, inc = rows < r0, cols < c0
        q = [[ext[s, ri, a * W:(a + 1) * W, b * W:(b + 1) * W] for b in range(2)] for a in range(2)]
        return jnp.where(inr, jnp.where(inc, q[1][1], q[1][0]), jnp.where(inc, q[0][1], q[0][0]))

    def phase_a(k, carry):
        pr, pi = probes[k, 0], probes[k, 1]
        ore, oim = pick(k, 0, 0), pick(k, 0, 1)
        a, b = forward(pr * ore - pi * oim, pr * oim + pi * ore, tables)
        wr, wi = inverse(freq_mul(a, kperm[0], False), freq_mul(b, kperm[1], False), tables)
        waves[k, 0] = wr
        waves[k, 1] = wi
        return carry

    def phase_b(k, carry):
        wr, wi = waves[k, 0], waves[k, 1]
        ore, oim = pick(k, 1, 0), pick(k, 1, 1)
        a, b = forward(wr * ore - wi * oim, wr * oim + wi * ore, tables)
        fa = a[:h] * a[:h] + a[h:] * a[h:] - mperm[k, :h, :]
        fb = b[:h] * b[:h] + b[h:] * b[h:] - mperm[k, h:, :]
        gr, gi = inverse(cat([fa * a[:h], fa * a[h:]], 0), cat([fb * b[:h], fb * b[h:]], 0), tables)
        wr, wi = waves[k, 0], waves[k, 1]
        grads[k, 0] = wr * gr + wi * gi
        grads[k, 1] = wr * gi - wi * gr
        ore, oim = pick(k, 1, 0), pick(k, 1, 1)
        waves[k, 0] = ore * gr + oim * gi
        waves[k, 1] = ore * gi - oim * gr
        return carry

    def phase_c(k, carry):
        a, b = forward(waves[k, 0], waves[k, 1], tables)
        gr, gi = inverse(freq_mul(a, kperm[0], True), freq_mul(b, kperm[1], True), tables)
        pr, pi = probes[k, 0], probes[k, 1]
        grads[k, 0] = pr * gr + pi * gi
        grads[k, 1] = pr * gi - pi * gr
        ore, oim = pick(k, 0, 0), pick(k, 0, 1)
        r0, c0 = start_of(k)
        used = k < count
        for i, x in enumerate((ore * gr + oim * gi, ore * gi - oim * gr)):
            x = turn(jnp.where(used, x, 0.0), lax.rem(W - r0, W), lax.rem(W - c0, W))
            psum[2 * i * W:(2 * i + 1) * W, :] += x[:, :h]
            psum[(2 * i + 1) * W:(2 * i + 2) * W, :] += x[:, h:]
        return carry

    def place(s):
        chunk_rows = lax.broadcasted_iota(jnp.int32, (CHUNK, W), 0)
        chunk_cols = lax.broadcasted_iota(jnp.int32, (CHUNK, W), 1)

        def one(at, carry):
            base = pl.multiple_of(at * CHUNK, CHUNK)
            inr = [chunk_rows < r0 - base for r0, c0 in starts]
            inc = [chunk_cols < c0 for r0, c0 in starts]
            used = [k < count for k in range(cap)]
            for ri in range(2):
                g = [jnp.where(used[k], grads[k, ri, pl.ds(base, CHUNK), :], 0.0) for k in range(cap)]
                high = [jnp.where(inr[k], g[k], 0.0) for k in range(cap)]
                for qa in range(2):
                    part = high if qa else [g[k] - high[k] for k in range(cap)]
                    far_side = [jnp.where(inc[k], part[k], 0.0) for k in range(cap)]
                    near_side = [part[k] - far_side[k] for k in range(cap)]
                    at_rows = pl.ds(pl.multiple_of(qa * W + base, CHUNK), CHUNK)
                    gext[s, ri, at_rows, pl.ds(0, W)] = sum(near_side[1:], near_side[0])
                    gext[s, ri, at_rows, pl.ds(W, W)] = sum(far_side[1:], far_side[0])
            return carry

        lax.fori_loop(0, W // CHUNK, one, 0)

    row_copies, col_copies = [], []
    for s in range(2):
        parts = []
        for at, (first, size) in enumerate(((0, h), (far, h), (h, W))):
            for d in range(2):
                n = s * 6 + at * 2 + d
                parts.append(remote(
                    gext.at[s, :, pl.ds(0, h) if d == 0 else pl.ds(far, h), pl.ds(first, size)],
                    rbuf.at[s, d, :, :, pl.ds(first, size)],
                    grow_send.at[n], grow_recv.at[n], to_up if d == 0 else to_down,
                ))
        row_copies.append(parts)
        sides = []
        for d in range(2):
            for side in range(2):
                n = s * 4 + d * 2 + side
                sides.append(remote(
                    gext.at[s, :, pl.ds(W, h) if d == 0 else pl.ds(h, h), pl.ds(0, h) if side == 0 else pl.ds(far, h)],
                    cbuf.at[s, d, side],
                    gcol_send.at[n], gcol_recv.at[n], to_left if side == 0 else to_right,
                ))
        col_copies.append(sides)

    def send_rows(s):
        for c in row_copies[s]:
            c.start()

    def send_cols(s):
        for d in range(2):
            at_rows = pl.ds(W, h) if d == 0 else pl.ds(h, h)
            for side in range(2):
                lanes = pl.ds(0, h) if side == 0 else pl.ds(far, h)
                row_copies[s][side * 2 + d].wait_recv()
                for ri in range(2):
                    gext[s, ri, at_rows, lanes] += rbuf[s, d, ri, :, lanes]
                col_copies[s][d * 2 + side].start()

    def finish_grad(s, mean):
        for d in range(2):
            row_copies[s][4 + d].wait_recv()
            q = 1 - d
            for side in range(2):
                col_copies[s][d * 2 + side].wait_recv()
                c = 1 - side
                lanes = pl.ds(h + c * h, h)
                for ri in range(2):
                    grad_out[s, ri, q * h:(q + 1) * h, c * h:(c + 1) * h] = (
                        gext[s, ri, pl.ds(h + q * h, h), lanes]
                        + rbuf[s, d, ri, :, lanes]
                        + cbuf[s, d, side, ri]
                    ) / mean

    psum[...] = jnp.zeros_like(psum)
    own.wait()
    forward_corners(0)
    finish_halo(0)
    lax.fori_loop(0, cap // 2, phase_a, 0)
    forward_corners(1)
    lax.fori_loop(cap // 2, cap, phase_a, 0)
    finish_halo(1)
    lax.fori_loop(0, cap, phase_b, 0)
    place(1)
    send_rows(1)
    lax.fori_loop(0, cap // 2, phase_c, 0)
    send_cols(1)
    lax.fori_loop(cap // 2, cap, phase_c, 0)
    place(0)
    send_rows(0)

    for j in range(NC):
        pieces[j, :piece_rows, :] = psum[j * piece_rows:(j + 1) * piece_rows, :]
        pieces[j, piece_rows:, :] = level

    def scatter_col(d):
        peer = lax.rem(col + d, NC)
        return remote(pieces.at[peer], landed.at[col], rs_send.at[d], rs_recv.at[d], (row, peer))

    def scatter_row(d):
        peer = lax.rem(row + d, NR)
        return remote(tiles.at[lax.div(peer, 2)], tile_landed.at[row], rt_send.at[d], rt_recv.at[d], (peer, col))

    def gather_row(d):
        z = lax.div(row, 2)
        peer = lax.rem(row + 2 * d, NR)
        return remote(tile_all.at[z], tile_all.at[z], ag_send.at[d], ag_recv.at[d], (peer, col))

    def gather_col(d):
        peer = lax.rem(col + d, NC)
        return remote(piece_all.at[col], piece_all.at[col], ac_send.at[d], ac_recv.at[d], (row, peer))

    def run(make, lo, hi, what):
        def step(d, carry):
            getattr(make(d), what)()
            return carry

        lax.fori_loop(lo, hi, step, 0)

    run(scatter_col, 1, NC, "start")
    landed[col] = pieces[col]
    send_cols(0)
    run(scatter_col, 1, NC, "wait_recv")
    got = landed[0]
    for j in range(1, NC):
        got = got + landed[j]
    for z in range(zs):
        tiles[z, :tile_rows, :] = got[z * tile_rows:(z + 1) * tile_rows]
        tiles[z, tile_rows:, :] = got[piece_rows:]
    run(scatter_row, 1, NR, "start")
    tile_landed[row] = tiles[lax.div(row, 2)]
    run(scatter_row, 1, NR, "wait_recv")
    got = tile_landed[0]
    for j in range(1, NR):
        got = got + tile_landed[j]
    total_all = got[tile_rows:tile_rows + 1, :1]
    scans = got[tile_rows + 4:tile_rows + 5, :1]
    mean = total_all / (scans * float(W * W))
    tile_all[lax.div(row, 2)] = got[:tile_rows] / (mean * scans)
    run(gather_row, 1, zs, "start")
    finish_grad(1, mean)
    run(gather_row, 1, zs, "wait_recv")
    for z in range(zs):
        piece_all[col, z * tile_rows:(z + 1) * tile_rows, :] = tile_all[z]
    run(gather_col, 1, NC, "start")
    finish_grad(0, mean)
    run(gather_col, 1, NC, "wait_recv")
    per_half = NC // 4
    for i in range(2):
        for half in range(2):
            for j in range(per_half):
                probe_out[i, j * piece_rows:(j + 1) * piece_rows, half * h:(half + 1) * h] = (
                    piece_all[(2 * i + half) * per_half + j]
                )
    for sides, middles, corners in halos:
        for c in sides + middles + corners:
            c.wait_send()
    for s in range(2):
        for c in row_copies[s] + col_copies[s]:
            c.wait_send()
    run(scatter_col, 1, NC, "wait_send")
    run(scatter_row, 1, NR, "wait_send")
    run(gather_row, 1, zs, "wait_send")
    run(gather_col, 1, NC, "wait_send")


def on_device(NR, NC, object_slices, probe_wave, propagator, measured, positions, scan_counts):
    W = probe_wave.shape[1]
    h = W // 2
    cap = measured.shape[2]
    zs = NR // 2
    piece_rows = 4 * W // NC
    tile_rows = piece_rows // zs
    vmem, smem = pl.BlockSpec(memory_space=pltpu.VMEM), pl.BlockSpec(memory_space=pltpu.SMEM)
    anywhere = pl.BlockSpec(memory_space=pl.ANY)
    V, D = pltpu.VMEM, pltpu.SemaphoreType.DMA
    return pl.pallas_call(
        functools.partial(kernel, W, NR, NC),
        out_shape=(
            jax.ShapeDtypeStruct((2, 2, W, W), F32),
            jax.ShapeDtypeStruct((2, W, W), F32),
        ),
        in_specs=[anywhere, vmem, vmem, vmem, smem, smem, vmem, vmem],
        out_specs=(vmem, vmem),
        scratch_shapes=[
            V((2, 2, 2 * W, 2 * W), F32),
            V((2, 2, 2 * W, 2 * W), F32),
            V((2, W, W), F32),
            V((cap, W, W), F32),
            V((cap, 2, W, W), F32),
            V((cap, 2, W, W), F32),
            V((cap, 2, W, W), F32),
            V((4 * W, h), F32),
            V((2, 2, 2, h, 2 * W), F32),
            V((2, 2, 2, 2, h, h), F32),
            V((NC, piece_rows + 8, h), F32),
            V((NC, piece_rows + 8, h), F32),
            V((zs, tile_rows + 8, h), F32),
            V((NR, tile_rows + 8, h), F32),
            V((zs, tile_rows, h), F32),
            V((NC, piece_rows, h), F32),
            D, D((20,)), D((20,)), D((12,)), D((12,)), D((8,)), D((8,)),
            D((NC,)), D((NC,)), D((NR,)), D((NR,)), D((zs,)), D((zs,)), D((NC,)), D((NC,)),
        ],
        compiler_params=pltpu.CompilerParams(
            collective_id=0, has_side_effects=True, vmem_limit_bytes=56 * 1024 * 1024
        ),
        name="ptychography",
    )(
        object_slices, probe_wave, propagator, measured[0, 0], positions.reshape(-1),
        scan_counts.reshape(-1), jnp.asarray(dft_tables(W)), jnp.asarray(order_tables(W)),
    )


def solution(mesh):
    placed = (
        P(None, None, "row", "col"),
        P(),
        P(),
        P("row", "col", None, None, None),
        P("row", "col", None, None),
        P("row", "col"),
    )
    return jax.shard_map(
        functools.partial(on_device, mesh.shape["row"], mesh.shape["col"]),
        mesh=mesh,
        in_specs=placed,
        out_specs=(P(None, None, "row", "col"), P()),
        check_vma=False,
    )
```

```python
import functools
import math

import jax
import jax.numpy as jnp
import ml_dtypes
import numpy as np
from jax import lax
from jax.experimental import pallas as pl
from jax.experimental.pallas import tpu as pltpu
from jax.sharding import PartitionSpec as P

F32, BF16 = jnp.float32, jnp.bfloat16
MESH = pl.DeviceIdType.MESH
EVEN, EVEN_T, ODD, ODD_T = 0, 2, 4, 6
CHUNK = 32


def split_table(table):
    high = table.astype(ml_dtypes.bfloat16)
    return [high, (table - high.astype(np.float64)).astype(ml_dtypes.bfloat16)]


def dft_tables(width):
    half = width // 2
    out = []
    for parity in range(2):
        k = np.arange(half)[:, None] * 2 + parity
        n = np.arange(half)[None, :]
        angle = 2.0 * math.pi * ((k * n) % width) / width
        c, s = np.cos(angle) / math.sqrt(width), np.sin(angle) / math.sqrt(width)
        block = np.block([[c, s], [-s, c]])
        out += split_table(block) + split_table(block.T)
    return np.stack(out)


def order_tables(width):
    half = width // 2
    order = np.concatenate([np.arange(half) * 2, np.arange(half) * 2 + 1])
    perm = np.zeros((width, width))
    perm[order, np.arange(width)] = 1.0
    return np.stack([perm, perm.T]).astype(ml_dtypes.bfloat16)


def cat(parts, axis):
    return jnp.concatenate(parts, axis=axis)


def split(x):
    high = x.astype(BF16)
    return high, (x - high.astype(F32)).astype(BF16)


def mm(a, b):
    return jnp.dot(a, b, preferred_element_type=F32)


def right(x, tables, at):
    high, low = split(x)
    th, tl = tables[at], tables[at + 1]
    return mm(high, th) + mm(low, th) + mm(high, tl)


def left(tables, at, x):
    high, low = split(x)
    th, tl = tables[at], tables[at + 1]
    return mm(th, high) + mm(th, low) + mm(tl, high)


def forward(fields, tables):
    h = fields[0][0].shape[1] // 2
    mid, out = [], []
    for re, im in fields:
        u = cat([re[:, :h] + re[:, h:], im[:, :h] + im[:, h:]], 1)
        v = cat([re[:, :h] - re[:, h:], im[:, :h] - im[:, h:]], 1)
        mid.append((right(u, tables, EVEN_T), right(v, tables, ODD_T)))
    for e, o in mid:
        es, os = e[:h] + e[h:], o[:h] + o[h:]
        ed, od = e[:h] - e[h:], o[:h] - o[h:]
        a = cat([cat([es[:, :h], os[:, :h]], 1), cat([es[:, h:], os[:, h:]], 1)], 0)
        b = cat([cat([ed[:, :h], od[:, :h]], 1), cat([ed[:, h:], od[:, h:]], 1)], 0)
        out.append((left(tables, EVEN, a), left(tables, ODD, b)))
    return out


def inverse(fields, tables):
    h = fields[0][0].shape[0] // 2
    mid, out = [], []
    for a, b in fields:
        mid.append((left(tables, EVEN_T, a), left(tables, ODD_T, b)))
    for e, o in mid:
        t, w = e + o, e - o
        qe = cat([cat([t[:h, :h], t[h:, :h]], 1), cat([w[:h, :h], w[h:, :h]], 1)], 0)
        qo = cat([cat([t[:h, h:], t[h:, h:]], 1), cat([w[:h, h:], w[h:, h:]], 1)], 0)
        e, o = right(qe, tables, EVEN), right(qo, tables, ODD)
        s, d = e + o, e - o
        out.append((cat([s[:, :h], d[:, :h]], 1), cat([s[:, h:], d[:, h:]], 1)))
    return out


def freq_mul(a, k, conj):
    h = a.shape[0] // 2
    kr, ki, ar, ai = k[:h], k[h:], a[:h], a[h:]
    if conj:
        return cat([kr * ar + ki * ai, kr * ai - ki * ar], 0)
    return cat([kr * ar - ki * ai, kr * ai + ki * ar], 0)


def reorder(x, order):
    high, low = split(x)
    high, low = split(mm(high, order[0]) + mm(low, order[0]))
    return mm(order[1], high) + mm(order[1], low)


def turn(x, down, along):
    return pltpu.roll(pltpu.roll(x, along, 1), down, 0)


def kernel(
    W, NR, NC,
    obj, probe_in, prop_in, meas_in, pos, cnt, tables_in, order_in,
    grad_out, probe_out,
    ext, gext, probe, prop, meas, tables, order, kperm, mperm, probes, patches, waves, grads, psum,
    rbuf, cbuf, swapped, landed, zbuf, piece_all, other, level_in,
    load_sem, halo_send, halo_recv, grow_send, grow_recv, gcol_send, gcol_recv,
    swap_sem, rs_send, rs_recv, rz_send, rz_recv, ac_send, ac_recv, lv_send, lv_recv,
):
    h = W // 2
    far = h + W
    cap = meas.shape[0]
    zs = NR // 2
    piece_rows = 2 * W // NC
    row, col = lax.axis_index("row"), lax.axis_index("col")
    core, z = lax.rem(row, 2), lax.div(row, 2)
    twin = (row + 1 - 2 * core, col)
    to_left, to_right = (row, lax.rem(col + NC - 1, NC)), (row, lax.rem(col + 1, NC))

    halves = [core, 1 - core]
    row_peers = [(lax.rem(row + NR + 2 * q - 1, NR), col) for q in halves]

    def span(start):
        return pl.ds(pl.multiple_of(start, h), h)

    def remote(src, dst, send, recv, device):
        return pltpu.make_async_remote_copy(
            src_ref=src, dst_ref=dst, send_sem=send, recv_sem=recv,
            device_id=device, device_id_type=MESH,
        )

    barrier = pltpu.get_barrier_semaphore()

    def greet(device):
        pl.semaphore_signal(barrier, inc=1, device_id=device, device_id_type=MESH)

    def greet_col(d, carry):
        greet((row, lax.rem(col + d, NC)))
        return carry

    def greet_row(d, carry):
        greet((lax.rem(row + 2 * d, NR), col))
        return carry

    for device in row_peers:
        greet(device)
    lax.fori_loop(1, NC, greet_col, 0)
    lax.fori_loop(1, zs, greet_row, 0)
    loads = [
        pltpu.make_async_copy(src, dst, load_sem.at[n])
        for n, (src, dst) in enumerate((
            (prop_in, prop), (order_in, order), (probe_in, probe), (meas_in, meas), (tables_in, tables),
            (obj, ext.at[:, :, h:far, h:far]),
        ))
    ]
    for c in loads:
        c.start()
    pl.semaphore_wait(barrier, NC + zs)

    halos = []
    for s in range(2):
        sides, middles, corners = [], [], []
        for t, q in enumerate(halves):
            for side in range(2):
                n = s * 10 + t * 2 + side
                lanes = pl.ds(0, h) if side == 0 else pl.ds(far, h)
                sides.append(remote(
                    obj.at[s, :, span(q * h), pl.ds(h, h) if side == 0 else pl.ds(0, h)],
                    ext.at[s, :, span(h + q * h), lanes],
                    halo_send.at[n], halo_recv.at[n], to_right if side == 0 else to_left,
                ))
                corners.append(remote(
                    ext.at[s, :, span(h + q * h), lanes],
                    ext.at[s, :, span((1 - q) * far), lanes],
                    halo_send.at[n + 4], halo_recv.at[n + 4], row_peers[t],
                ))
            n = s * 10 + 8 + t
            middles.append(remote(
                obj.at[s, :, span(q * h), :],
                ext.at[s, :, span((1 - q) * far), pl.ds(h, W)],
                halo_send.at[n], halo_recv.at[n], row_peers[t],
            ))
        halos.append((sides, middles, corners))
    for sides, middles, corners in halos:
        for c in sides + middles:
            c.start()

    def forward_corners(s):
        sides, middles, corners = halos[s]
        for side, corner in zip(sides, corners):
            side.wait_recv()
            corner.start()

    def finish_halo(s):
        sides, middles, corners = halos[s]
        for c in middles + corners:
            c.wait_recv()

    rows = lax.broadcasted_iota(jnp.int32, (W, W), 0)
    cols = lax.broadcasted_iota(jnp.int32, (W, W), 1)
    count = cnt[0]

    def start_of(k):
        return jnp.clip(pos[0, k] + h, 0, W), jnp.clip(pos[1, k] + h, 0, W)

    def prepare(k, total):
        r0, c0 = start_of(k)
        m = meas[k]
        mperm[k] = reorder(m, order)
        probes[k, 0] = turn(probe[0], lax.rem(r0, W), lax.rem(c0, W))
        probes[k, 1] = turn(probe[1], lax.rem(r0, W), lax.rem(c0, W))
        return total + jnp.where(k < count, jnp.sum(m.reshape(W // 8, 8, W), axis=0), 0.0)

    def pick(k, s, ri):
        r0, c0 = start_of(k)
        inr, inc = rows < r0, cols < c0
        q = [[ext[s, ri, a * W:(a + 1) * W, b * W:(b + 1) * W] for b in range(2)] for a in range(2)]
        return jnp.where(inr, jnp.where(inc, q[1][1], q[1][0]), jnp.where(inc, q[0][1], q[0][0]))

    def pair(i):
        return [2 * i, 2 * i + 1]

    def phase_a(i, carry):
        exits = []
        for k in pair(i):
            pr, pi = probes[k, 0], probes[k, 1]
            ore, oim = pick(k, 0, 0), pick(k, 0, 1)
            patches[k, 0] = ore
            patches[k, 1] = oim
            exits.append((pr * ore - pi * oim, pr * oim + pi * ore))
        far_fields = forward(exits, tables)
        far_fields = [
            (freq_mul(a, kperm[0], False), freq_mul(b, kperm[1], False)) for a, b in far_fields
        ]
        for k, (wr, wi) in zip(pair(i), inverse(far_fields, tables)):
            waves[k, 0] = wr
            waves[k, 1] = wi
        return carry

    def phase_b(i, carry):
        exits, objects = [], []
        for k in pair(i):
            wr, wi = waves[k, 0], waves[k, 1]
            ore, oim = pick(k, 1, 0), pick(k, 1, 1)
            objects.append((ore, oim))
            exits.append((wr * ore - wi * oim, wr * oim + wi * ore))
        scaled = []
        for k, (a, b) in zip(pair(i), forward(exits, tables)):
            fa = a[:h] * a[:h] + a[h:] * a[h:] - mperm[k, :h, :]
            fb = b[:h] * b[:h] + b[h:] * b[h:] - mperm[k, h:, :]
            scaled.append((cat([fa * a[:h], fa * a[h:]], 0), cat([fb * b[:h], fb * b[h:]], 0)))
        for k, (ore, oim), (gr, gi) in zip(pair(i), objects, inverse(scaled, tables)):
            wr, wi = waves[k, 0], waves[k, 1]
            grads[k, 0] = jnp.where(k < count, wr * gr + wi * gi, 0.0)
            grads[k, 1] = jnp.where(k < count, wr * gi - wi * gr, 0.0)
            waves[k, 0] = ore * gr + oim * gi
            waves[k, 1] = ore * gi - oim * gr
        return carry

    def phase_c(i, carry):
        far_fields = forward([(waves[k, 0], waves[k, 1]) for k in pair(i)], tables)
        far_fields = [
            (freq_mul(a, kperm[0], True), freq_mul(b, kperm[1], True)) for a, b in far_fields
        ]
        for k, (gr, gi) in zip(pair(i), inverse(far_fields, tables)):
            used = k < count
            r0, c0 = start_of(k)
            pr, pi = probes[k, 0], probes[k, 1]
            grads[k, 0] = jnp.where(used, pr * gr + pi * gi, 0.0)
            grads[k, 1] = jnp.where(used, pr * gi - pi * gr, 0.0)
            ore, oim = patches[k, 0], patches[k, 1]
            for n, x in enumerate((ore * gr + oim * gi, ore * gi - oim * gr)):
                x = turn(jnp.where(used, x, 0.0), lax.rem(W - r0, W), lax.rem(W - c0, W))
                psum[n, :W, :] += x[:, :h]
                psum[n, W:2 * W, :] += x[:, h:]
        return carry

    def place(s):
        chunk_rows = lax.broadcasted_iota(jnp.int32, (CHUNK, W), 0)
        chunk_cols = lax.broadcasted_iota(jnp.int32, (CHUNK, W), 1)

        def one(at, carry):
            base = pl.multiple_of(at * CHUNK, CHUNK)
            starts = [start_of(k) for k in range(cap)]
            inr = [chunk_rows < r0 - base for r0, c0 in starts]
            inc = [chunk_cols < c0 for r0, c0 in starts]
            for ri in range(2):
                g = [grads[k, ri, pl.ds(base, CHUNK), :] for k in range(cap)]
                high = [jnp.where(inr[k], g[k], 0.0) for k in range(cap)]
                for qa in range(2):
                    part = high if qa else [g[k] - high[k] for k in range(cap)]
                    far_side = [jnp.where(inc[k], part[k], 0.0) for k in range(cap)]
                    near_side = [part[k] - far_side[k] for k in range(cap)]
                    at_rows = pl.ds(pl.multiple_of(qa * W + base, CHUNK), CHUNK)
                    gext[s, ri, at_rows, pl.ds(0, W)] = sum(near_side[1:], near_side[0])
                    gext[s, ri, at_rows, pl.ds(W, W)] = sum(far_side[1:], far_side[0])
            return carry

        lax.fori_loop(0, W // CHUNK, one, 0)

    def share_levels(d):
        return remote(level_in.at[col], level_in.at[col], lv_send.at[d], lv_recv.at[d], (row, lax.rem(col + d, NC)))

    row_copies, col_copies = [], []
    for s in range(2):
        edges, centres, sides = [], [], []
        for t, q in enumerate(halves):
            for at, (first, size) in enumerate(((0, h), (far, h), (h, W))):
                n = s * 6 + t * 3 + at
                (centres if at == 2 else edges).append(remote(
                    gext.at[s, :, span(q * far), pl.ds(first, size)],
                    rbuf.at[s, t, :, :, pl.ds(first, size)],
                    grow_send.at[n], grow_recv.at[n], row_peers[t],
                ))
            for side in range(2):
                n = s * 4 + t * 2 + side
                sides.append(remote(
                    gext.at[s, :, span(h + q * h), pl.ds(0, h) if side == 0 else pl.ds(far, h)],
                    cbuf.at[s, t, side],
                    gcol_send.at[n], gcol_recv.at[n], to_left if side == 0 else to_right,
                ))
        row_copies.append((edges, centres))
        col_copies.append(sides)

    def send_rows(s):
        for c in row_copies[s][0] + row_copies[s][1]:
            c.start()

    def send_cols(s):
        for t, q in enumerate(halves):
            for side in range(2):
                lanes = pl.ds(0, h) if side == 0 else pl.ds(far, h)
                row_copies[s][0][t * 2 + side].wait_recv()
                for ri in range(2):
                    gext[s, ri, span(h + q * h), lanes] += rbuf[s, t, ri, :, lanes]
                col_copies[s][t * 2 + side].start()

    def finish_grad(s, mean):
        for t, q in enumerate(halves):
            row_copies[s][1][t].wait_recv()
            for side in range(2):
                col_copies[s][t * 2 + side].wait_recv()
                c = 1 - side
                lanes = pl.ds(h + c * h, h)
                for ri in range(2):
                    grad_out[s, ri, span(q * h), c * h:(c + 1) * h] = (
                        gext[s, ri, span(h + q * h), lanes]
                        + rbuf[s, t, ri, :, lanes]
                        + cbuf[s, t, side, ri]
                    ) / mean

    def split_planes():
        return remote(psum.at[1 - core], swapped, swap_sem.at[0], swap_sem.at[1], twin)

    def scatter_col(d):
        peer = lax.rem(col + d, NC)
        src = psum.at[core, pl.ds(pl.multiple_of(peer * piece_rows, piece_rows), piece_rows), :]
        return remote(src, landed.at[col], rs_send.at[d], rs_recv.at[d], (row, peer))

    def share_z(d):
        return remote(zbuf.at[z], zbuf.at[z], rz_send.at[d], rz_recv.at[d], (lax.rem(row + 2 * d, NR), col))

    def gather_col(d):
        return remote(piece_all.at[col], piece_all.at[col], ac_send.at[d], ac_recv.at[d], (row, lax.rem(col + d, NC)))

    def join_planes():
        return remote(piece_all, other, swap_sem.at[2], swap_sem.at[3], twin)

    def run(make, hi, what):
        def step(d, carry):
            getattr(make(d), what)()
            return carry

        lax.fori_loop(1, hi, step, 0)

    psum[...] = jnp.zeros_like(psum)
    for c in loads[:2]:
        c.wait()
    kr, ki = reorder(prop[0], order), reorder(prop[1], order)
    kperm[0] = cat([kr[:h], ki[:h]], 0)
    kperm[1] = cat([kr[h:], ki[h:]], 0)
    for c in loads[2:4]:
        c.wait()
    total = jnp.sum(lax.fori_loop(0, cap, prepare, jnp.zeros((8, W), F32)))
    first_rows = lax.broadcasted_iota(jnp.int32, (8, h), 0) < 4
    level_in[col] = jnp.where(first_rows, total, count.astype(F32))
    run(share_levels, NC, "start")
    for c in loads[4:]:
        c.wait()
    forward_corners(0)
    finish_halo(0)
    lax.fori_loop(0, cap // 4, phase_a, 0)
    forward_corners(1)
    lax.fori_loop(cap // 4, cap // 2, phase_a, 0)
    run(share_levels, NC, "wait_recv")
    got = level_in[0]
    for j in range(1, NC):
        got = got + level_in[j]
    psum[0, 2 * W:, :] = got
    psum[1, 2 * W:, :] = got
    finish_halo(1)
    lax.fori_loop(0, cap // 4, phase_b, 0)
    lax.fori_loop(cap // 4, cap // 2, phase_b, 0)
    place(1)
    send_rows(1)
    lax.fori_loop(0, cap // 4, phase_c, 0)
    lax.fori_loop(cap // 4, cap // 2, phase_c, 0)
    split_planes().start()
    place(0)
    send_rows(0)
    split_planes().wait_recv()
    psum[core] += swapped[...]
    run(scatter_col, NC, "start")
    send_cols(1)
    landed[col] = psum[core, pl.ds(pl.multiple_of(col * piece_rows, piece_rows), piece_rows), :]
    run(scatter_col, NC, "wait_recv")
    got = landed[0]
    for j in range(1, NC):
        got = got + landed[j]
    zbuf[z, :piece_rows, :] = got
    zbuf[z, piece_rows:, :] = psum[core, 2 * W:, :]
    run(share_z, zs, "start")
    send_cols(0)
    run(share_z, zs, "wait_recv")
    got = zbuf[0]
    for j in range(1, zs):
        got = got + zbuf[j]
    scans = got[piece_rows + 4:piece_rows + 5, :1]
    mean = got[piece_rows:piece_rows + 1, :1] / (scans * float(W * W))
    piece_all[col] = got[:piece_rows] / (mean * scans)
    run(gather_col, NC, "start")
    finish_grad(1, mean)
    finish_grad(0, mean)
    run(gather_col, NC, "wait_recv")
    join_planes().start()
    per_half = NC // 2
    for half in range(2):
        for j in range(per_half):
            probe_out[core, j * piece_rows:(j + 1) * piece_rows, half * h:(half + 1) * h] = (
                piece_all[half * per_half + j]
            )
    join_planes().wait_recv()
    for half in range(2):
        for j in range(per_half):
            probe_out[1 - core, j * piece_rows:(j + 1) * piece_rows, half * h:(half + 1) * h] = (
                other[half * per_half + j]
            )
    for sides, middles, corners in halos:
        for c in sides + middles + corners:
            c.wait_send()
    for s in range(2):
        for c in row_copies[s][0] + row_copies[s][1] + col_copies[s]:
            c.wait_send()
    for c in [split_planes(), join_planes()]:
        c.wait_send()
    run(share_levels, NC, "wait_send")
    run(scatter_col, NC, "wait_send")
    run(share_z, zs, "wait_send")
    run(gather_col, NC, "wait_send")


def on_device(NR, NC, object_slices, probe_wave, propagator, measured, positions, scan_counts):
    W = probe_wave.shape[1]
    h = W // 2
    cap = measured.shape[2]
    zs = NR // 2
    piece_rows = 2 * W // NC
    vmem, smem = pl.BlockSpec(memory_space=pltpu.VMEM), pl.BlockSpec(memory_space=pltpu.SMEM)
    anywhere = pl.BlockSpec(memory_space=pl.ANY)
    V, D = pltpu.VMEM, pltpu.SemaphoreType.DMA
    return pl.pallas_call(
        functools.partial(kernel, W, NR, NC),
        out_shape=(
            pltpu.VMEM((2, 2, W, W), F32),
            pltpu.VMEM((2, W, W), F32),
        ),
        in_specs=[anywhere] * 4 + [smem] * 2 + [anywhere] * 2,
        out_specs=(vmem, vmem),
        scratch_shapes=[
            V((2, 2, 2 * W, 2 * W), F32),
            V((2, 2, 2 * W, 2 * W), F32),
            V((2, W, W), F32),
            V((2, W, W), F32),
            V((cap, W, W), F32),
            V((8, W, W), BF16),
            V((2, W, W), BF16),
            V((2, W, W), F32),
            V((cap, W, W), F32),
            V((cap, 2, W, W), F32),
            V((cap, 2, W, W), F32),
            V((cap, 2, W, W), F32),
            V((cap, 2, W, W), F32),
            V((2, 2 * W + 8, h), F32),
            V((2, 2, 2, h, 2 * W), F32),
            V((2, 2, 2, 2, h, h), F32),
            V((2 * W + 8, h), F32),
            V((NC, piece_rows, h), F32),
            V((zs, piece_rows + 8, h), F32),
            V((NC, piece_rows, h), F32),
            V((NC, piece_rows, h), F32),
            V((NC, 8, h), F32),
            D((6,)), D((20,)), D((20,)), D((12,)), D((12,)), D((8,)), D((8,)),
            D((4,)), D((NC,)), D((NC,)), D((zs,)), D((zs,)), D((NC,)), D((NC,)),
            D((NC,)), D((NC,)),
        ],
        compiler_params=pltpu.CompilerParams(
            collective_id=0, has_side_effects=True, vmem_limit_bytes=56 * 1024 * 1024
        ),
        name="ptychography",
    )(
        object_slices, probe_wave, propagator, measured[0, 0], positions[0, 0].T,
        scan_counts[0], jnp.asarray(dft_tables(W)), jnp.asarray(order_tables(W)),
    )


def solution(mesh):
    placed = (
        P(None, None, "row", "col"),
        P(),
        P(),
        P("row", "col", None, None, None),
        P("row", "col", None, None),
        P("row", "col"),
    )
    return jax.shard_map(
        functools.partial(on_device, mesh.shape["row"], mesh.shape["col"]),
        mesh=mesh,
        in_specs=placed,
        out_specs=(P(None, None, "row", "col"), P()),
        check_vma=False,
    )
```

```python
import functools
import math

import jax
import jax.numpy as jnp
import ml_dtypes
import numpy as np
from jax import lax
from jax.experimental import pallas as pl
from jax.experimental.pallas import tpu as pltpu
from jax.sharding import PartitionSpec as P

F32, BF16 = jnp.float32, jnp.bfloat16
MESH = pl.DeviceIdType.MESH
EVEN, EVEN_T, ODD, ODD_T = 0, 2, 4, 6
CHUNK = 32


def split_table(table):
    high = table.astype(ml_dtypes.bfloat16)
    return [high, (table - high.astype(np.float64)).astype(ml_dtypes.bfloat16)]


def dft_tables(width):
    half = width // 2
    out = []
    for parity in range(2):
        k = np.arange(half)[:, None] * 2 + parity
        n = np.arange(half)[None, :]
        angle = 2.0 * math.pi * ((k * n) % width) / width
        c, s = np.cos(angle) / math.sqrt(width), np.sin(angle) / math.sqrt(width)
        block = np.block([[c, s], [-s, c]])
        out += split_table(block) + split_table(block.T)
    return np.stack(out)


def order_tables(width):
    half = width // 2
    order = np.concatenate([np.arange(half) * 2, np.arange(half) * 2 + 1])
    perm = np.zeros((width, width))
    perm[order, np.arange(width)] = 1.0
    return np.stack([perm, perm.T]).astype(ml_dtypes.bfloat16)


def cat(parts, axis):
    return jnp.concatenate(parts, axis=axis)


def split(x):
    high = x.astype(BF16)
    return high, (x - high.astype(F32)).astype(BF16)


def mm(a, b):
    return jnp.dot(a, b, preferred_element_type=F32)


def right(x, tables, at):
    high, low = split(x)
    th, tl = tables[at], tables[at + 1]
    return mm(high, th) + mm(low, th) + mm(high, tl)


def left(tables, at, x):
    high, low = split(x)
    th, tl = tables[at], tables[at + 1]
    return mm(th, high) + mm(th, low) + mm(tl, high)


def forward(fields, tables):
    h = fields[0][0].shape[1] // 2
    mid, out = [], []
    for re, im in fields:
        u = cat([re[:, :h] + re[:, h:], im[:, :h] + im[:, h:]], 1)
        v = cat([re[:, :h] - re[:, h:], im[:, :h] - im[:, h:]], 1)
        mid.append((right(u, tables, EVEN_T), right(v, tables, ODD_T)))
    for e, o in mid:
        es, os = e[:h] + e[h:], o[:h] + o[h:]
        ed, od = e[:h] - e[h:], o[:h] - o[h:]
        a = cat([cat([es[:, :h], os[:, :h]], 1), cat([es[:, h:], os[:, h:]], 1)], 0)
        b = cat([cat([ed[:, :h], od[:, :h]], 1), cat([ed[:, h:], od[:, h:]], 1)], 0)
        out.append((left(tables, EVEN, a), left(tables, ODD, b)))
    return out


def inverse(fields, tables):
    h = fields[0][0].shape[0] // 2
    mid, out = [], []
    for a, b in fields:
        mid.append((left(tables, EVEN_T, a), left(tables, ODD_T, b)))
    for e, o in mid:
        t, w = e + o, e - o
        qe = cat([cat([t[:h, :h], t[h:, :h]], 1), cat([w[:h, :h], w[h:, :h]], 1)], 0)
        qo = cat([cat([t[:h, h:], t[h:, h:]], 1), cat([w[:h, h:], w[h:, h:]], 1)], 0)
        e, o = right(qe, tables, EVEN), right(qo, tables, ODD)
        s, d = e + o, e - o
        out.append((cat([s[:, :h], d[:, :h]], 1), cat([s[:, h:], d[:, h:]], 1)))
    return out


def freq_mul(a, k, conj):
    h = a.shape[0] // 2
    kr, ki, ar, ai = k[:h], k[h:], a[:h], a[h:]
    if conj:
        return cat([kr * ar + ki * ai, kr * ai - ki * ar], 0)
    return cat([kr * ar - ki * ai, kr * ai + ki * ar], 0)


def reorder(x, order):
    high, low = split(x)
    high, low = split(mm(high, order[0]) + mm(low, order[0]))
    return mm(order[1], high) + mm(order[1], low)


def turn(x, down, along):
    return pltpu.roll(pltpu.roll(x, along, 1), down, 0)


def kernel(
    W, NR, NC,
    obj, probe_in, prop_in, meas_in, pos, cnt, tables_in, order_in,
    grad_out, probe_out,
    ext, gext, probe, prop, meas, tables, order, kperm, mperm, probes, patches, waves, grads, psum,
    rbuf, cbuf, swapped, landed, zbuf, piece_all, other, level_in,
    load_sem, halo_send, halo_recv, grow_send, grow_recv, gcol_send, gcol_recv,
    swap_sem, rs_send, rs_recv, rz_send, rz_recv, ac_send, ac_recv, lv_send, lv_recv,
):
    h = W // 2
    far = h + W
    cap = meas.shape[0]
    zs = NR // 2
    piece_rows = 2 * W // NC
    row, col = lax.axis_index("row"), lax.axis_index("col")
    core, z = lax.rem(row, 2), lax.div(row, 2)
    twin = (row + 1 - 2 * core, col)
    to_left, to_right = (row, lax.rem(col + NC - 1, NC)), (row, lax.rem(col + 1, NC))

    halves = [core, 1 - core]
    row_peers = [(lax.rem(row + NR + 2 * q - 1, NR), col) for q in halves]

    def span(start):
        return pl.ds(pl.multiple_of(start, h), h)

    def remote(src, dst, send, recv, device):
        return pltpu.make_async_remote_copy(
            src_ref=src, dst_ref=dst, send_sem=send, recv_sem=recv,
            device_id=device, device_id_type=MESH,
        )

    barrier = pltpu.get_barrier_semaphore()

    def greet(device):
        pl.semaphore_signal(barrier, inc=1, device_id=device, device_id_type=MESH)

    def greet_col(d, carry):
        greet((row, lax.rem(col + d, NC)))
        return carry

    def greet_row(d, carry):
        greet((lax.rem(row + 2 * d, NR), col))
        return carry

    for device in row_peers:
        greet(device)
    lax.fori_loop(1, NC, greet_col, 0)
    lax.fori_loop(1, zs, greet_row, 0)
    loads = [
        pltpu.make_async_copy(src, dst, load_sem.at[n])
        for n, (src, dst) in enumerate((
            (prop_in, prop), (order_in, order), (probe_in, probe), (meas_in, meas), (tables_in, tables),
            (obj, ext.at[:, :, h:far, h:far]),
        ))
    ]
    for c in loads:
        c.start()
    pl.semaphore_wait(barrier, NC + zs)

    halos = []
    for s in range(2):
        sides, middles, corners = [], [], []
        for t, q in enumerate(halves):
            for side in range(2):
                n = s * 10 + t * 2 + side
                lanes = pl.ds(0, h) if side == 0 else pl.ds(far, h)
                sides.append(remote(
                    obj.at[s, :, span(q * h), pl.ds(h, h) if side == 0 else pl.ds(0, h)],
                    ext.at[s, :, span(h + q * h), lanes],
                    halo_send.at[n], halo_recv.at[n], to_right if side == 0 else to_left,
                ))
                corners.append(remote(
                    ext.at[s, :, span(h + q * h), lanes],
                    ext.at[s, :, span((1 - q) * far), lanes],
                    halo_send.at[n + 4], halo_recv.at[n + 4], row_peers[t],
                ))
            n = s * 10 + 8 + t
            middles.append(remote(
                obj.at[s, :, span(q * h), :],
                ext.at[s, :, span((1 - q) * far), pl.ds(h, W)],
                halo_send.at[n], halo_recv.at[n], row_peers[t],
            ))
        halos.append((sides, middles, corners))
    for sides, middles, corners in halos:
        for c in sides + middles:
            c.start()

    def forward_corners(s):
        sides, middles, corners = halos[s]
        for side, corner in zip(sides, corners):
            side.wait_recv()
            corner.start()

    def finish_halo(s):
        sides, middles, corners = halos[s]
        for c in middles + corners:
            c.wait_recv()

    rows = lax.broadcasted_iota(jnp.int32, (W, W), 0)
    cols = lax.broadcasted_iota(jnp.int32, (W, W), 1)
    count = cnt[0]

    def start_of(k):
        return jnp.clip(pos[0, k] + h, 0, W), jnp.clip(pos[1, k] + h, 0, W)

    def prepare(k, total):
        r0, c0 = start_of(k)
        m = meas[k]
        mperm[k] = reorder(m, order)
        probes[k, 0] = turn(probe[0], lax.rem(r0, W), lax.rem(c0, W))
        probes[k, 1] = turn(probe[1], lax.rem(r0, W), lax.rem(c0, W))
        return total + jnp.where(k < count, jnp.sum(m.reshape(W // 8, 8, W), axis=0), 0.0)

    def pick(k, s, ri):
        r0, c0 = start_of(k)
        inr, inc = rows < r0, cols < c0
        q = [[ext[s, ri, a * W:(a + 1) * W, b * W:(b + 1) * W] for b in range(2)] for a in range(2)]
        return jnp.where(inr, jnp.where(inc, q[1][1], q[1][0]), jnp.where(inc, q[0][1], q[0][0]))

    def pair(i):
        return [2 * i, 2 * i + 1]

    def phase_a(i, carry):
        exits = []
        for k in pair(i):
            pr, pi = probes[k, 0], probes[k, 1]
            ore, oim = pick(k, 0, 0), pick(k, 0, 1)
            patches[k, 0] = ore
            patches[k, 1] = oim
            exits.append((pr * ore - pi * oim, pr * oim + pi * ore))
        far_fields = forward(exits, tables)
        far_fields = [
            (freq_mul(a, kperm[0], False), freq_mul(b, kperm[1], False)) for a, b in far_fields
        ]
        for k, (wr, wi) in zip(pair(i), inverse(far_fields, tables)):
            waves[k, 0] = wr
            waves[k, 1] = wi
        return carry

    def phase_b(i, carry):
        exits, objects = [], []
        for k in pair(i):
            wr, wi = waves[k, 0], waves[k, 1]
            ore, oim = pick(k, 1, 0), pick(k, 1, 1)
            objects.append((ore, oim))
            exits.append((wr * ore - wi * oim, wr * oim + wi * ore))
        scaled = []
        for k, (a, b) in zip(pair(i), forward(exits, tables)):
            fa = a[:h] * a[:h] + a[h:] * a[h:] - mperm[k, :h, :]
            fb = b[:h] * b[:h] + b[h:] * b[h:] - mperm[k, h:, :]
            scaled.append((cat([fa * a[:h], fa * a[h:]], 0), cat([fb * b[:h], fb * b[h:]], 0)))
        for k, (ore, oim), (gr, gi) in zip(pair(i), objects, inverse(scaled, tables)):
            wr, wi = waves[k, 0], waves[k, 1]
            grads[k, 0] = jnp.where(k < count, wr * gr + wi * gi, 0.0)
            grads[k, 1] = jnp.where(k < count, wr * gi - wi * gr, 0.0)
            waves[k, 0] = ore * gr + oim * gi
            waves[k, 1] = ore * gi - oim * gr
        return carry

    def phase_c(i, carry):
        far_fields = forward([(waves[k, 0], waves[k, 1]) for k in pair(i)], tables)
        far_fields = [
            (freq_mul(a, kperm[0], True), freq_mul(b, kperm[1], True)) for a, b in far_fields
        ]
        for k, (gr, gi) in zip(pair(i), inverse(far_fields, tables)):
            used = k < count
            r0, c0 = start_of(k)
            pr, pi = probes[k, 0], probes[k, 1]
            grads[k, 0] = jnp.where(used, pr * gr + pi * gi, 0.0)
            grads[k, 1] = jnp.where(used, pr * gi - pi * gr, 0.0)
            ore, oim = patches[k, 0], patches[k, 1]
            for n, x in enumerate((ore * gr + oim * gi, ore * gi - oim * gr)):
                x = turn(jnp.where(used, x, 0.0), lax.rem(W - r0, W), lax.rem(W - c0, W))
                psum[n, :W, :] += x[:, :h]
                psum[n, W:2 * W, :] += x[:, h:]
        return carry

    def place(s):
        chunk_rows = lax.broadcasted_iota(jnp.int32, (CHUNK, W), 0)
        chunk_cols = lax.broadcasted_iota(jnp.int32, (CHUNK, W), 1)

        def one(at, carry):
            base = pl.multiple_of(at * CHUNK, CHUNK)
            starts = [start_of(k) for k in range(cap)]
            inr = [chunk_rows < r0 - base for r0, c0 in starts]
            inc = [chunk_cols < c0 for r0, c0 in starts]
            for ri in range(2):
                g = [grads[k, ri, pl.ds(base, CHUNK), :] for k in range(cap)]
                high = [jnp.where(inr[k], g[k], 0.0) for k in range(cap)]
                for qa in range(2):
                    part = high if qa else [g[k] - high[k] for k in range(cap)]
                    far_side = [jnp.where(inc[k], part[k], 0.0) for k in range(cap)]
                    near_side = [part[k] - far_side[k] for k in range(cap)]
                    at_rows = pl.ds(pl.multiple_of(qa * W + base, CHUNK), CHUNK)
                    gext[s, ri, at_rows, pl.ds(0, W)] = sum(near_side[1:], near_side[0])
                    gext[s, ri, at_rows, pl.ds(W, W)] = sum(far_side[1:], far_side[0])
            return carry

        lax.fori_loop(0, W // CHUNK, one, 0)

    def share_levels(d):
        return remote(level_in.at[col], level_in.at[col], lv_send.at[d], lv_recv.at[d], (row, lax.rem(col + d, NC)))

    row_copies, col_copies = [], []
    for s in range(2):
        edges, centres, sides = [], [], []
        for t, q in enumerate(halves):
            for at, (first, size) in enumerate(((0, h), (far, h), (h, W))):
                n = s * 6 + t * 3 + at
                (centres if at == 2 else edges).append(remote(
                    gext.at[s, :, span(q * far), pl.ds(first, size)],
                    rbuf.at[s, t, :, :, pl.ds(first, size)],
                    grow_send.at[n], grow_recv.at[n], row_peers[t],
                ))
            for side in range(2):
                n = s * 4 + t * 2 + side
                sides.append(remote(
                    gext.at[s, :, span(h + q * h), pl.ds(0, h) if side == 0 else pl.ds(far, h)],
                    cbuf.at[s, t, side],
                    gcol_send.at[n], gcol_recv.at[n], to_left if side == 0 else to_right,
                ))
        row_copies.append((edges, centres))
        col_copies.append(sides)

    def send_rows(s):
        for c in row_copies[s][0] + row_copies[s][1]:
            c.start()

    def send_cols(s):
        for t, q in enumerate(halves):
            for side in range(2):
                lanes = pl.ds(0, h) if side == 0 else pl.ds(far, h)
                row_copies[s][0][t * 2 + side].wait_recv()
                for ri in range(2):
                    gext[s, ri, span(h + q * h), lanes] += rbuf[s, t, ri, :, lanes]
                col_copies[s][t * 2 + side].start()

    def finish_grad(s, mean):
        for t, q in enumerate(halves):
            row_copies[s][1][t].wait_recv()
            for side in range(2):
                col_copies[s][t * 2 + side].wait_recv()
                c = 1 - side
                lanes = pl.ds(h + c * h, h)
                for ri in range(2):
                    grad_out[s, ri, span(q * h), c * h:(c + 1) * h] = (
                        gext[s, ri, span(h + q * h), lanes]
                        + rbuf[s, t, ri, :, lanes]
                        + cbuf[s, t, side, ri]
                    ) / mean

    def split_planes():
        return remote(psum.at[1 - core], swapped, swap_sem.at[0], swap_sem.at[1], twin)

    def scatter_col(d):
        peer = lax.rem(col + d, NC)
        src = psum.at[core, pl.ds(pl.multiple_of(peer * piece_rows, piece_rows), piece_rows), :]
        return remote(src, landed.at[col], rs_send.at[d], rs_recv.at[d], (row, peer))

    def share_z(d):
        return remote(zbuf.at[z], zbuf.at[z], rz_send.at[d], rz_recv.at[d], (lax.rem(row + 2 * d, NR), col))

    def gather_col(d):
        return remote(piece_all.at[col], piece_all.at[col], ac_send.at[d], ac_recv.at[d], (row, lax.rem(col + d, NC)))

    def join_planes():
        return remote(piece_all, other, swap_sem.at[2], swap_sem.at[3], twin)

    def run(make, hi, what):
        def step(d, carry):
            getattr(make(d), what)()
            return carry

        lax.fori_loop(1, hi, step, 0)

    psum[...] = jnp.zeros_like(psum)
    for c in loads[:2]:
        c.wait()
    kr, ki = reorder(prop[0], order), reorder(prop[1], order)
    kperm[0] = cat([kr[:h], ki[:h]], 0)
    kperm[1] = cat([kr[h:], ki[h:]], 0)
    for c in loads[2:4]:
        c.wait()
    total = jnp.sum(lax.fori_loop(0, cap, prepare, jnp.zeros((8, W), F32)))
    first_rows = lax.broadcasted_iota(jnp.int32, (8, h), 0) < 4
    level_in[col] = jnp.where(first_rows, total, count.astype(F32))
    run(share_levels, NC, "start")
    for c in loads[4:]:
        c.wait()
    forward_corners(0)
    finish_halo(0)
    lax.fori_loop(0, cap // 4, phase_a, 0)
    forward_corners(1)
    lax.fori_loop(cap // 4, cap // 2, phase_a, 0)
    run(share_levels, NC, "wait_recv")
    got = level_in[0]
    for j in range(1, NC):
        got = got + level_in[j]
    psum[0, 2 * W:, :] = got
    psum[1, 2 * W:, :] = got
    finish_halo(1)
    lax.fori_loop(0, cap // 4, phase_b, 0)
    lax.fori_loop(cap // 4, cap // 2, phase_b, 0)
    place(1)
    send_rows(1)
    lax.fori_loop(0, cap // 4, phase_c, 0)
    lax.fori_loop(cap // 4, cap // 2, phase_c, 0)
    split_planes().start()
    split_planes().wait_recv()
    psum[core] += swapped[...]
    run(scatter_col, NC, "start")
    send_cols(1)
    place(0)
    send_rows(0)
    landed[col] = psum[core, pl.ds(pl.multiple_of(col * piece_rows, piece_rows), piece_rows), :]
    run(scatter_col, NC, "wait_recv")
    got = landed[0]
    for j in range(1, NC):
        got = got + landed[j]
    zbuf[z, :piece_rows, :] = got
    zbuf[z, piece_rows:, :] = psum[core, 2 * W:, :]
    run(share_z, zs, "start")
    send_cols(0)
    run(share_z, zs, "wait_recv")
    got = zbuf[0]
    for j in range(1, zs):
        got = got + zbuf[j]
    scans = got[piece_rows + 4:piece_rows + 5, :1]
    mean = got[piece_rows:piece_rows + 1, :1] / (scans * float(W * W))
    piece_all[col] = got[:piece_rows] / (mean * scans)
    run(gather_col, NC, "start")
    finish_grad(1, mean)
    finish_grad(0, mean)
    run(gather_col, NC, "wait_recv")
    join_planes().start()
    per_half = NC // 2
    for half in range(2):
        for j in range(per_half):
            probe_out[core, j * piece_rows:(j + 1) * piece_rows, half * h:(half + 1) * h] = (
                piece_all[half * per_half + j]
            )
    join_planes().wait_recv()
    for half in range(2):
        for j in range(per_half):
            probe_out[1 - core, j * piece_rows:(j + 1) * piece_rows, half * h:(half + 1) * h] = (
                other[half * per_half + j]
            )
    for sides, middles, corners in halos:
        for c in sides + middles + corners:
            c.wait_send()
    for s in range(2):
        for c in row_copies[s][0] + row_copies[s][1] + col_copies[s]:
            c.wait_send()
    for c in [split_planes(), join_planes()]:
        c.wait_send()
    run(share_levels, NC, "wait_send")
    run(scatter_col, NC, "wait_send")
    run(share_z, zs, "wait_send")
    run(gather_col, NC, "wait_send")


def on_device(NR, NC, object_slices, probe_wave, propagator, measured, positions, scan_counts):
    W = probe_wave.shape[1]
    h = W // 2
    cap = measured.shape[2]
    zs = NR // 2
    piece_rows = 2 * W // NC
    vmem, smem = pl.BlockSpec(memory_space=pltpu.VMEM), pl.BlockSpec(memory_space=pltpu.SMEM)
    anywhere = pl.BlockSpec(memory_space=pl.ANY)
    V, D = pltpu.VMEM, pltpu.SemaphoreType.DMA
    return pl.pallas_call(
        functools.partial(kernel, W, NR, NC),
        out_shape=(
            pltpu.VMEM((2, 2, W, W), F32),
            pltpu.VMEM((2, W, W), F32),
        ),
        in_specs=[anywhere] * 4 + [smem] * 2 + [anywhere] * 2,
        out_specs=(vmem, vmem),
        scratch_shapes=[
            V((2, 2, 2 * W, 2 * W), F32),
            V((2, 2, 2 * W, 2 * W), F32),
            V((2, W, W), F32),
            V((2, W, W), F32),
            V((cap, W, W), F32),
            V((8, W, W), BF16),
            V((2, W, W), BF16),
            V((2, W, W), F32),
            V((cap, W, W), F32),
            V((cap, 2, W, W), F32),
            V((cap, 2, W, W), F32),
            V((cap, 2, W, W), F32),
            V((cap, 2, W, W), F32),
            V((2, 2 * W + 8, h), F32),
            V((2, 2, 2, h, 2 * W), F32),
            V((2, 2, 2, 2, h, h), F32),
            V((2 * W + 8, h), F32),
            V((NC, piece_rows, h), F32),
            V((zs, piece_rows + 8, h), F32),
            V((NC, piece_rows, h), F32),
            V((NC, piece_rows, h), F32),
            V((NC, 8, h), F32),
            D((6,)), D((20,)), D((20,)), D((12,)), D((12,)), D((8,)), D((8,)),
            D((4,)), D((NC,)), D((NC,)), D((zs,)), D((zs,)), D((NC,)), D((NC,)),
            D((NC,)), D((NC,)),
        ],
        compiler_params=pltpu.CompilerParams(
            collective_id=0, has_side_effects=True, vmem_limit_bytes=56 * 1024 * 1024
        ),
        name="ptychography",
    )(
        object_slices, probe_wave, propagator, measured[0, 0], positions[0, 0].T,
        scan_counts[0], jnp.asarray(dft_tables(W)), jnp.asarray(order_tables(W)),
    )


def solution(mesh):
    placed = (
        P(None, None, "row", "col"),
        P(),
        P(),
        P("row", "col", None, None, None),
        P("row", "col", None, None),
        P("row", "col"),
    )
    return jax.shard_map(
        functools.partial(on_device, mesh.shape["row"], mesh.shape["col"]),
        mesh=mesh,
        in_specs=placed,
        out_specs=(P(None, None, "row", "col"), P()),
        check_vma=False,
    )
```
